32 devices in a mesh: grp: 4 (over x, core), rep: 8 (over z, y).
Axes of the slice: x: 2, y: 2, z: 4, core: 2. Of those that a mesh axis runs over, the one named last changes fastest.
Arguments:
- inputs: float32 [8, 1024, 1024], P('rep', 'grp'), may hold values from -6 to 6
- project_in: bfloat16 [2, 1024, 3072], P(None, 'grp'), may hold values from -0.1875 to 0.1875
- project_out: bfloat16 [2, 1024, 1024], P(None, 'grp'), may hold values from -3 to 3
- expand: bfloat16 [2, 1024, 4096], P(None, 'grp'), may hold values from -0.1875 to 0.1875
- contract: bfloat16 [2, 4096, 1024], P(None, 'grp'), may hold values from -0.09375 to 0.09375
- norm_gain: bfloat16 [2, 2, 1024], P(None, None, 'grp'), may hold values from 0.5 to 1.5
- norm_shift: bfloat16 [2, 2, 1024], P(None, None, 'grp'), may hold values from -4 to 4
- branch_bias: bfloat16 [2, 4, 1024], P(None, None, 'grp'), may hold values from -4 to 4
- expand_bias: bfloat16 [2, 4096], P(None, 'grp'), may hold values from -4 to 4
- cotangent: float32 [8, 1024, 1024], P('rep', 'grp'), may hold values from -6 to 6
Outputs:
- activations: float32 [8, 1024, 1024], P('rep', 'grp')
- input_grad: float32 [8, 1024, 1024], P('rep', 'grp')
- inproj_grad: float32 [2, 1024, 3072], P(None, 'grp')
- outproj_grad: float32 [2, 1024, 1024], P(None, 'grp')
- expand_grad: float32 [2, 1024, 4096], P(None, 'grp')
- contract_grad: float32 [2, 4096, 1024], P(None, 'grp')
- gain_grad: float32 [2, 2, 1024], P(None, None, 'grp')
- shift_grad: float32 [2, 2, 1024], P(None, None, 'grp')
- bias_grad: float32 [2, 4, 1024], P(None, None, 'grp')
- upbias_grad: float32 [2, 4096], P(None, 'grp')
The draws below stay inside these ranges and needn't reach their ends.
All inputs are finite; a program needn't handle non-finite values.
Results may differ from the reference program's by a relative error of at most 0.015.
Values may be sent and summed in bfloat16 or wider, within the bound.
No kernel may reach another device: no remote copies, remote signals or barrier semaphores. Data moves between devices by JAX's collectives and lax.ppermute only.
A program may use at most 320 MiB of HBM per device.

```python
import math
import jax
import jax.numpy as jnp
from jax import lax

D = 1024
FF = 4096
HEADS = 16
HEAD = 64
LAYERS = 2
LEN = 1024
SEQS = 8


def levels(stream_key, dims, split, smallest, high):
    factor_of, own = 1.0, jax.random.fold_in(stream_key, 6)
    for position, shards_of in split:
        steps = jnp.exp(jax.random.uniform(jax.random.fold_in(own, position), (shards_of,), jnp.float32, smallest / len(split), high / len(split)))
        factor_of = factor_of * jnp.repeat(steps, dims[position] // shards_of).reshape([-1 if axis == position else 1 for axis in range(len(dims))])
    return factor_of


def scatter_about(key, shape, deviation, reach, cuts=(), kind=jnp.bfloat16):
    array = deviation * jax.random.normal(key, shape, jnp.float32)
    if cuts:
        array = array * levels(key, shape, cuts, -0.22, 0.18)
    return jnp.clip(array, -reach, reach).astype(kind)


def setup_inputs(seed: int = 0) -> dict:
    arg_keys = jax.random.split(jax.random.key(seed), 11)
    inputs = scatter_about(arg_keys[0], (SEQS, LEN, D), 1.0, 6.0, ((0, 8), (1, 4)), jnp.float32)
    project_in = scatter_about(arg_keys[1], (LAYERS, D, 3 * D), D ** -0.5, 0.1875, ((1, 4),))
    project_out = scatter_about(arg_keys[2], (LAYERS, D, D), (D * 4 // LEN) ** -0.5, 3.0, ((1, 4),))
    expand = scatter_about(arg_keys[3], (LAYERS, D, FF), D ** -0.5, 0.1875, ((1, 4),))
    contract = scatter_about(arg_keys[4], (LAYERS, FF, D), FF ** -0.5, 0.09375, ((1, 4),))
    norm_gain = jnp.clip(1.0 + 0.1 * jax.random.normal(arg_keys[5], (LAYERS, 2, D), jnp.float32), 0.5, 1.5).astype(jnp.bfloat16)
    norm_shift = scatter_about(arg_keys[6], (LAYERS, 2, D), 0.3, 4.0, ((2, 4),))
    branch_bias = scatter_about(arg_keys[7], (LAYERS, 4, D), 0.5, 4.0, ((2, 4),))
    expand_bias = scatter_about(arg_keys[8], (LAYERS, FF), 0.5, 4.0, ((1, 4),))
    cotangent = scatter_about(arg_keys[9], (SEQS, LEN, D), 1.0, 6.0, ((0, 8), (1, 4)), jnp.float32)
    return {"inputs": inputs, "project_in": project_in, "project_out": project_out, "expand": expand, "contract": contract, "norm_gain": norm_gain, "norm_shift": norm_shift, "branch_bias": branch_bias, "expand_bias": expand_bias, "cotangent": cotangent}


@jax.custom_vjp
def low(v):
    return lax.optimization_barrier(v.astype(jnp.bfloat16)).astype(jnp.float32)

@jax.custom_vjp
def low_back(v):
    return v

def low_keep(v):
    return (low(v), None)

def low_pass(kept, grad):
    return (grad,)

def back_keep(v):
    return (v, None)

def back_low(kept, grad):
    return (low(grad),)
low.defvjp(low_keep, low_pass)
low_back.defvjp(back_keep, back_low)

def normalize(values, gain, shift):
    average = lax.optimization_barrier(jnp.mean(values, -1, keepdims=True))
    centered = values - average
    spread = lax.optimization_barrier(jnp.mean(centered * centered, -1, keepdims=True))
    return centered * lax.rsqrt(spread + 1e-05) * gain + shift

def attend(queries, keys, values):
    block_rows = min(512, LEN)
    blocks = LEN // block_rows
    factor = HEAD ** (-0.5)
    grouped = queries.reshape(HEADS, blocks, block_rows, HEAD).transpose(1, 0, 2, 3)
    starts = jnp.arange(blocks, dtype=jnp.int32) * block_rows
    positions = jnp.arange(LEN, dtype=jnp.int32)

    def one_block(pair):
        block, start = pair
        scores = jnp.einsum('hqd,hkd->hqk', block, keys, precision=lax.Precision.HIGHEST) * factor
        scores = low_back(scores)
        rowpos = start + jnp.arange(block_rows, dtype=jnp.int32)
        causal = positions[None, :] <= rowpos[:, None]
        scores = jnp.where(causal[None], scores, -1e+30)
        top = lax.optimization_barrier(jnp.max(scores, -1, keepdims=True))
        exponent = jnp.exp(scores - top)
        weights = low(exponent / lax.optimization_barrier(jnp.sum(exponent, -1, keepdims=True)))
        return jnp.einsum('hqk,hkd->hqd', weights, values, precision=lax.Precision.HIGHEST)
    result = lax.map(jax.checkpoint(one_block), (grouped, starts))
    return result.transpose(1, 0, 2, 3).reshape(HEADS, LEN, HEAD)

def layer_forward(hidden, input_projection, output_projection, widen_projection, narrow_projection, gains, shifts, bias_vectors, widen_bias):
    count = hidden.shape[0]
    first_norm_output = low(normalize(hidden, gains[0], shifts[0]))
    token_offset = jnp.concatenate([bias_vectors[0], jnp.zeros_like(bias_vectors[0]), bias_vectors[1]])
    mixed_tokens = jnp.einsum('cqw,wr->cqr', first_norm_output, input_projection, precision=lax.Precision.HIGHEST) + token_offset
    mixed_tokens = low_back(low(mixed_tokens))

    def heads_of(part):
        return part.reshape(count, LEN, HEADS, HEAD).transpose(0, 2, 1, 3)
    queries = heads_of(mixed_tokens[..., :D])
    keys = heads_of(mixed_tokens[..., D:2 * D])
    values = heads_of(mixed_tokens[..., 2 * D:])
    attended_tokens = jax.vmap(attend)(queries, keys, values)
    attended_tokens = low_back(low(attended_tokens.transpose(0, 2, 1, 3).reshape(count, LEN, D)))
    branch_output = low_back(jnp.einsum('cqw,wr->cqr', attended_tokens, output_projection, precision=lax.Precision.HIGHEST) + bias_vectors[2])
    middle = hidden + branch_output
    second_norm_output = low(normalize(middle, gains[1], shifts[1]))
    raised_units = low_back(jnp.einsum('epy,yb->epb', second_norm_output, widen_projection, precision=lax.Precision.HIGHEST) + widen_bias)
    active_units = low(jax.nn.gelu(raised_units, approximate=True))
    block_output = low_back(jnp.einsum('ghb,bk->ghk', active_units, narrow_projection, precision=lax.Precision.HIGHEST) + bias_vectors[3])
    return middle + block_output

def stacked_forward(hidden, weights):
    for index in range(LAYERS):
        hidden = layer_forward(hidden, *[item[index] for item in weights])
    return hidden

def reference(inputs, project_in, project_out, expand, contract, norm_gain, norm_shift, branch_bias, expand_bias, cotangent):
    weights = tuple((item.astype(jnp.float32) for item in (project_in, project_out, expand, contract, norm_gain, norm_shift, branch_bias, expand_bias)))
    group = math.gcd(SEQS, max(1, 4096 // LEN))
    rounds = SEQS // group
    pieces = inputs.astype(jnp.float32).reshape(rounds, group, LEN, D)
    grads_in = cotangent.astype(jnp.float32).reshape(rounds, group, LEN, D)

    def one_round(totals, pair):
        piece, incoming = pair
        block_output, pull = jax.vjp(stacked_forward, piece, weights)
        back_input, back_weights = pull(incoming)
        totals = tuple((earlier + latest for earlier, latest in zip(totals, back_weights)))
        return (totals, (block_output, back_input))
    zeros = tuple((jnp.zeros(item.shape, jnp.float32) for item in weights))
    totals, (outputs, back_inputs) = lax.scan(one_round, zeros, (pieces, grads_in))
    return (outputs.reshape(SEQS, LEN, D), back_inputs.reshape(SEQS, LEN, D), totals[0], totals[1], totals[2], totals[3], totals[4], totals[5], totals[6], totals[7])
```

```python
import functools

import jax
import jax.numpy as jnp
from jax import lax
from jax.experimental import pallas as pl
from jax.experimental.pallas import tpu as pltpu
from jax.sharding import PartitionSpec as P

HEADS = 16
LANES = 128
F32 = jnp.float32
BF16 = jnp.bfloat16


def swap(value, flip):
    count = lax.axis_size("grp")
    return lax.ppermute(value, "grp", [(i, i ^ flip) for i in range(count)])


def spread(block):
    far = swap(block, 2)
    near = swap(block, 1)
    return jnp.concatenate([block, near, far, swap(far, 1)], 0)


def collect(parts):
    rows = parts.shape[0] // 4
    parts = parts.reshape(4, rows, parts.shape[1])
    got_far = swap(parts[3], 1)
    far = (parts[2].astype(F32) + got_far.astype(F32)).astype(BF16)
    got = swap(far, 2)
    near = swap(parts[1], 1)
    return parts[0].astype(F32) + near.astype(F32) + got.astype(F32)


def place_blocks(blocks, me):
    out = jnp.zeros((len(blocks),) + blocks[0].shape, blocks[0].dtype)
    for r, block in enumerate(blocks):
        out = lax.dynamic_update_index_in_dim(out, block, me ^ r, 0)
    return out


def exchange(value, me):
    got = []
    for r in range(4):
        piece = lax.dynamic_index_in_dim(value, me ^ r, 0, keepdims=False)
        got.append(swap(piece, r) if r else piece)
    return place_blocks(got, me)


def stages(count):
    sizes = {8: (2, 4), 32: (4, 2, 4)}.get(count, (count,))
    out, stride = [], 1
    for size in sizes:
        out.append((stride, size))
        stride *= size
    return out


def ring(value, stride, size):
    count = lax.axis_size("rep")
    pairs = []
    for i in range(count):
        here = (i // stride) % size
        pairs.append((i, i + ((here + 1) % size - here) * stride))
    return lax.ppermute(value, "rep", pairs)


def place_of(stride, size):
    return lax.rem(lax.div(lax.axis_index("rep"), stride), size)


def scatter_stage(value, axis, stride, size):
    here = place_of(stride, size)

    def chunk(index):
        return lax.dynamic_index_in_dim(value, index, axis, keepdims=False)

    moving = chunk(lax.rem(here + size - 1, size))
    for step in range(1, size):
        moving = ring(moving, stride, size)
        own = chunk(lax.rem(here + 2 * size - 1 - step, size))
        moving = (moving.astype(F32) + own.astype(F32)).astype(BF16)
    return moving


def gather_stage(value, axis, stride, size):
    here = place_of(stride, size)
    out = jnp.zeros(value.shape[:axis] + (size,) + value.shape[axis:], value.dtype)
    out = lax.dynamic_update_index_in_dim(out, value, here, axis)
    moving = value
    for step in range(1, size):
        moving = ring(moving, stride, size)
        out = lax.dynamic_update_index_in_dim(out, moving, lax.rem(here + size - step, size), axis)
    return out


def replica_sum(value, turn, slow_first):
    count = lax.axis_size("rep")
    parts = stages(count)
    if slow_first:
        parts = parts[::-1]
    lead, rows, columns = value.shape
    sizes = [size for _, size in parts]
    value = value.reshape([lead] + sizes + [rows // count, columns])
    for stride, size in parts:
        value = scatter_stage(value, 1, stride, size)
    value = turn(value)
    for stride, size in parts[::-1]:
        value = gather_stage(value, 1, stride, size)
    return value.reshape((value.shape[0], rows) + value.shape[-1:])


def total_small(value):
    for flip in (1, 2):
        value = value + swap(value, flip)
    count = lax.axis_size("rep")
    flip = 1
    while flip < count:
        value = value + lax.ppermute(value, "rep", [(i, i ^ flip) for i in range(count)])
        flip *= 2
    return value


def dot(a, b, contract):
    return lax.dot_general(a, b, ((contract[:1], contract[1:]), ((), ())), preferred_element_type=F32)


def attend_kernel(me_ref, mixed_ref, out_ref, *, width, head, rows, blocks):
    me = me_ref[0]
    scale = head**-0.5
    which = lax.broadcasted_iota(jnp.int32, (rows, LANES), 1) // head
    below = lax.broadcasted_iota(jnp.int32, (rows, rows), 1) <= lax.broadcasted_iota(
        jnp.int32, (rows, rows), 0
    )
    for pair in range(width // LANES):
        column = pair * LANES

        def block(index, part):
            start = pl.multiple_of((me ^ index) * rows, rows)
            return mixed_ref[pl.ds(start, rows), part * width + column : part * width + column + LANES]

        keys = [block(j, 1) for j in range(blocks)]
        values = [block(j, 2) for j in range(blocks)]
        for i in range(blocks):
            query = block(i, 0) * jnp.asarray(scale, BF16)
            result = jnp.zeros((rows, LANES), F32)
            for h in range(LANES // head):
                mine = jnp.where(which == h, query, jnp.zeros_like(query))
                scores = [dot(mine, keys[j], (1, 1)) for j in range(i + 1)]
                scores[i] = jnp.where(below, scores[i], -1e30)
                top = functools.reduce(
                    jnp.maximum, [jnp.max(s, 1, keepdims=True) for s in scores]
                )
                exps = [jnp.exp(s - top) for s in scores]
                total = sum(jnp.sum(e, 1, keepdims=True) for e in exps)
                acc = sum(dot(e.astype(BF16), values[j], (1, 0)) for j, e in enumerate(exps))
                result = jnp.where(which == h, acc / total, result)
            start = pl.multiple_of((me ^ i) * rows, rows)
            out_ref[pl.ds(start, rows), column : column + LANES] = result.astype(BF16)


def attend_back_kernel(me_ref, mixed_ref, grad_ref, out_ref, *, width, head, rows, blocks):
    me = me_ref[0]
    scale = head**-0.5
    which = lax.broadcasted_iota(jnp.int32, (rows, LANES), 1) // head
    above = lax.broadcasted_iota(jnp.int32, (rows, rows), 0) <= lax.broadcasted_iota(
        jnp.int32, (rows, rows), 1
    )
    for pair in range(width // LANES):
        column = pair * LANES

        def place(index):
            return pl.ds(pl.multiple_of((me ^ index) * rows, rows), rows)

        def block(index, part):
            return mixed_ref[place(index), part * width + column : part * width + column + LANES]

        keys = [block(j, 1) for j in range(blocks)]
        values = [block(j, 2) for j in range(blocks)]
        d_keys = [jnp.zeros((rows, LANES), F32) for _ in range(blocks)]
        d_values = [jnp.zeros((rows, LANES), F32) for _ in range(blocks)]
        for i in range(blocks):
            query = block(i, 0) * jnp.asarray(scale, BF16)
            grad = grad_ref[place(i), column : column + LANES]
            d_query = jnp.zeros((rows, LANES), F32)
            for h in range(LANES // head):
                mine = jnp.where(which == h, query, jnp.zeros_like(query))
                mine_grad = jnp.where(which == h, grad, jnp.zeros_like(grad))
                scores = [dot(keys[j], mine, (1, 1)) for j in range(i + 1)]
                scores[i] = jnp.where(above, scores[i], -1e30)
                top = functools.reduce(
                    jnp.maximum, [jnp.max(s, 0, keepdims=True) for s in scores]
                )
                exps = [jnp.exp(s - top) for s in scores]
                inverse = 1.0 / sum(jnp.sum(e, 0, keepdims=True) for e in exps)
                probs = [e * inverse for e in exps]
                d_probs = [dot(values[j], mine_grad, (1, 1)) for j in range(i + 1)]
                inner = sum(jnp.sum(p * g, 0, keepdims=True) for p, g in zip(probs, d_probs))
                found = jnp.zeros((rows, LANES), F32)
                for j in range(i + 1):
                    d_score = (probs[j] * (d_probs[j] - inner)).astype(BF16)
                    d_keys[j] = d_keys[j] + dot(d_score, mine, (1, 0))
                    d_values[j] = d_values[j] + dot(probs[j].astype(BF16), mine_grad, (1, 0))
                    found = found + dot(d_score, keys[j], (0, 0))
                d_query = jnp.where(which == h, found, d_query)
            out_ref[place(i), column : column + LANES] = (d_query * scale).astype(BF16)
        for j in range(blocks):
            out_ref[place(j), width + column : width + column + LANES] = d_keys[j].astype(BF16)
            out_ref[place(j), 2 * width + column : 2 * width + column + LANES] = d_values[j].astype(BF16)


def attention(me, mixed, head, blocks, grad=None):
    length, triple = mixed.shape
    width = triple // 3
    sizes = dict(width=width, head=head, rows=length // blocks, blocks=blocks)
    heads = width // head
    half = length * length // 2
    if grad is None:
        kernel, arrays, out_width, products = attend_kernel, (mixed,), width, 2
    else:
        kernel, arrays, out_width, products = attend_back_kernel, (mixed, grad), triple, 5
    return pl.pallas_call(
        functools.partial(kernel, **sizes),
        out_shape=jax.ShapeDtypeStruct((length, out_width), BF16),
        in_specs=[pl.BlockSpec(memory_space=pltpu.SMEM)]
        + [pl.BlockSpec(memory_space=pltpu.VMEM)] * len(arrays),
        out_specs=pl.BlockSpec(memory_space=pltpu.VMEM),
        compiler_params=pltpu.CompilerParams(vmem_limit_bytes=40 * 2**20),
        cost_estimate=pl.CostEstimate(
            flops=products * 2 * half * heads * LANES * 2,
            bytes_accessed=length * triple * 4,
            transcendentals=half * heads,
        ),
    )(jnp.reshape(me, (1,)).astype(jnp.int32), *arrays)


def normed(values):
    average = jnp.mean(values, -1, keepdims=True)
    centered = values - average
    spread_of = jnp.mean(centered * centered, -1, keepdims=True)
    rate = lax.rsqrt(spread_of + 1e-05)
    return centered * rate, rate


def norm_back(incoming, values, gain):
    hat, rate = normed(values)
    scaled = incoming * gain
    first = jnp.mean(scaled, -1, keepdims=True)
    second = jnp.mean(scaled * hat, -1, keepdims=True)
    d_gain = jnp.sum(incoming * hat, 0)
    d_shift = jnp.sum(incoming, 0)
    return rate * (scaled - first - hat * second), d_gain, d_shift


def gelu_tanh(values):
    return jax.nn.gelu(values, approximate=True)


def shards(
    inputs,
    project_in,
    project_out,
    expand,
    contract,
    norm_gain,
    norm_shift,
    branch_bias,
    expand_bias,
    cotangent,
):
    layers = project_in.shape[0]
    rows, width = inputs.shape[1:]
    groups = lax.axis_size("grp")
    replicas = lax.axis_size("rep")
    head = width // HEADS
    part = width // groups
    hidden_part = expand.shape[2] // groups
    me = lax.axis_index("grp")
    replica = lax.axis_index("rep")

    def columns_by_device(weight, pieces):
        count = weight.shape[0]
        cut = weight.reshape(count, pieces, groups, -1)
        return cut.transpose(2, 0, 1, 3).reshape(groups, count, -1)

    in_columns = [None] * layers
    up_columns = [None] * layers
    in_columns[0] = exchange(columns_by_device(project_in[0], 3), me).reshape(width, 3 * part)
    slice_rows = part // replicas

    def slice_of(weight):
        return lax.dynamic_slice_in_dim(weight, replica * slice_rows, slice_rows, 0)

    wanted = []
    for index in range(layers):
        if index:
            wanted.append(("in", index, columns_by_device(slice_of(project_in[index]), 3)))
        wanted.append(("up", index, columns_by_device(slice_of(expand[index]), 1)))
    packed = exchange(jnp.concatenate([item[2] for item in wanted], -1), me)
    start = 0
    for kind, index, item in wanted:
        size = item.shape[-1]
        piece = packed[:, :, start : start + size]
        start += size
        whole = lax.all_gather(piece, "rep", axis=1, tiled=True).reshape(width, size)
        (in_columns if kind == "in" else up_columns)[index] = whole

    small = jnp.concatenate([norm_gain, norm_shift, branch_bias[:, 2:]], 1)
    small = lax.all_gather(small, "grp", axis=2, tiled=True).astype(F32)
    gains, shifts, out_biases = small[:, 0:2], small[:, 2:4], small[:, 4:6]
    mix_bias = jnp.concatenate(
        [branch_bias[:, 0], jnp.zeros_like(branch_bias[:, 0]), branch_bias[:, 1]], -1
    ).astype(F32)
    up_bias = expand_bias.astype(F32)

    state = inputs[0]
    saved = []
    for index in range(layers):
        hat, _ = normed(state)
        first = spread((hat * gains[index, 0] + shifts[index, 0]).astype(BF16))
        mixed = (dot(first, in_columns[index], (1, 0)) + mix_bias[index]).astype(BF16)
        attended = attention(me, mixed, head, groups)
        branch = dot(attended, project_out[index], (1, 0)).astype(BF16)
        middle = state + collect(branch) + out_biases[index, 0]
        hat, _ = normed(middle)
        second = spread((hat * gains[index, 1] + shifts[index, 1]).astype(BF16))
        raised = dot(second, up_columns[index], (1, 0)) + up_bias[index]
        active = gelu_tanh(raised).astype(BF16)
        down = dot(active, contract[index], (1, 0)).astype(BF16)
        saved.append((state, first, mixed, attended, middle, second, raised.astype(BF16), active))
        state = middle + collect(down) + out_biases[index, 1]

    grad = cotangent[0]
    grads = [None] * layers
    smalls = [None] * layers

    def keep(value):
        return value

    def turn_columns(pieces):
        def turn(value):
            got = exchange(value, me)
            count = got.shape[1]
            got = got.reshape(groups, count, pieces, -1).transpose(1, 2, 0, 3)
            return got.reshape(1, count, -1)

        return turn

    for index in reversed(range(layers)):
        before, first, mixed, attended, middle, second, raised, active = saved[index]
        d_down_own = grad.astype(BF16)
        d_down = spread(d_down_own)
        d_active = dot(d_down, contract[index], (1, 1))
        pull = jax.vjp(gelu_tanh, raised.astype(F32))[1]
        d_raised = pull(d_active)[0].astype(BF16)
        d_second = collect(dot(d_raised, up_columns[index], (1, 1)).astype(BF16))
        g_contract = dot(active, d_down, (0, 0)).astype(BF16)
        g_contract = replica_sum(g_contract[None], keep, False)[0]
        g_expand = dot(second, d_raised, (0, 0)).astype(BF16)
        g_expand = replica_sum(g_expand.reshape(groups, part, hidden_part), turn_columns(1), False)[0]
        d_up_bias = jnp.sum(d_raised.astype(F32), 0)
        d_middle, d_gain_two, d_shift_two = norm_back(d_second, middle, gains[index, 1])
        d_middle = grad + d_middle
        d_branch_own = d_middle.astype(BF16)
        d_branch = spread(d_branch_own)
        d_attended = dot(d_branch, project_out[index], (1, 1)).astype(BF16)
        d_mixed = attention(me, mixed, head, groups, d_attended)
        d_first = collect(dot(d_mixed, in_columns[index], (1, 1)).astype(BF16))
        g_out = dot(attended, d_branch, (0, 0)).astype(BF16)
        g_out = replica_sum(g_out[None], keep, True)[0]
        g_in = dot(first, d_mixed, (0, 0)).astype(BF16)
        g_in = replica_sum(g_in.reshape(groups, part, 3 * part), turn_columns(3), False)[0]
        d_mix_bias = jnp.sum(d_mixed.astype(F32), 0)
        d_first, d_gain_one, d_shift_one = norm_back(d_first, before, gains[index, 0])
        own_rows = [
            d_gain_one,
            d_gain_two,
            d_shift_one,
            d_shift_two,
            jnp.sum(d_branch_own.astype(F32), 0),
            jnp.sum(d_down_own.astype(F32), 0),
        ]
        own_part = jnp.concatenate([d_mix_bias[:part], d_mix_bias[2 * part :], d_up_bias])
        grads[index] = (g_in, g_out, g_expand, g_contract)
        smalls[index] = (jnp.stack(own_rows), own_part)
        grad = d_middle + d_first

    whole = jnp.stack([item[0] for item in smalls])
    owned = jnp.stack([item[1] for item in smalls])
    owned_all = jnp.zeros((groups,) + owned.shape, F32)
    owned_all = lax.dynamic_update_index_in_dim(owned_all, owned, me, 0)
    summed = total_small(jnp.concatenate([whole.reshape(-1), owned_all.reshape(-1)]))
    whole = summed[: whole.size].reshape(whole.shape)
    whole = lax.dynamic_slice_in_dim(whole, me * part, part, 2)
    owned = lax.dynamic_index_in_dim(
        summed[-owned_all.size :].reshape(owned_all.shape), me, 0, keepdims=False
    )
    merged = [
        jnp.stack([grads[index][member] for index in range(layers)]).astype(F32)
        for member in range(4)
    ]
    bias_grad = jnp.concatenate(
        [owned[:, None, :part], owned[:, None, part : 2 * part], whole[:, 4:6]], 1
    )
    return (
        state[None],
        grad[None],
        merged[0],
        merged[1],
        merged[2],
        merged[3],
        whole[:, 0:2],
        whole[:, 2:4],
        bias_grad,
        owned[:, 2 * part :],
    )


def solution(mesh):
    placed = (
        P("rep", "grp", None),
        P(None, "grp", None),
        P(None, "grp", None),
        P(None, "grp", None),
        P(None, "grp", None),
        P(None, None, "grp"),
        P(None, None, "grp"),
        P(None, None, "grp"),
        P(None, "grp"),
        P("rep", "grp", None),
    )
    return jax.shard_map(
        shards,
        mesh=mesh,
        in_specs=placed,
        out_specs=(
            P("rep", "grp", None),
            P("rep", "grp", None),
            P(None, "grp", None),
            P(None, "grp", None),
            P(None, "grp", None),
            P(None, "grp", None),
            P(None, None, "grp"),
            P(None, None, "grp"),
            P(None, None, "grp"),
            P(None, "grp"),
        ),
        check_vma=False,
    )
```

```python
import functools
import math

import jax
import jax.numpy as jnp
from jax import lax
from jax.experimental import pallas as pl
from jax.experimental.pallas import tpu as pltpu
from jax.sharding import PartitionSpec as P

HEADS = 16
LANES = 128
F32 = jnp.float32
BF16 = jnp.bfloat16


def swap(value, flip):
    count = lax.axis_size("grp")
    return lax.ppermute(value, "grp", [(i, i ^ flip) for i in range(count)])


def spread(block):
    far = swap(block, 2)
    near = swap(block, 1)
    return jnp.concatenate([block, near, far, swap(far, 1)], 0)


def collect(parts):
    rows = parts.shape[0] // 4
    parts = parts.reshape(4, rows, parts.shape[1])
    got_far = swap(parts[3], 1)
    far = (parts[2].astype(F32) + got_far.astype(F32)).astype(BF16)
    got = swap(far, 2)
    near = swap(parts[1], 1)
    return parts[0].astype(F32) + near.astype(F32) + got.astype(F32)


def exchange(value, me):
    got = [
        swap(lax.dynamic_index_in_dim(value, me ^ r, 0, keepdims=False), r)
        for r in range(1, lax.axis_size("grp"))
    ]
    got = yield got
    out = value
    for r, block in enumerate(got, 1):
        out = lax.dynamic_update_index_in_dim(out, block, me ^ r, 0)
    return out


def at_once(task):
    try:
        got = next(task)
        while True:
            got = task.send(got)
    except StopIteration as end:
        return end.value


def cross(value, bit):
    count = lax.axis_size("rep")
    return lax.ppermute(value, "rep", [(i, i ^ bit) for i in range(count)])


def tied(values, anchor):
    if anchor is None:
        return values
    return list(lax.optimization_barrier(tuple(values) + (anchor,))[:-1])


def replica_bits():
    count = lax.axis_size("rep")
    bits = [1]
    while 2 * bits[-1] < count:
        bits.append(2 * bits[-1])
    return bits


def replica_sum(value, turn, order):
    here = lax.axis_index("rep")
    chunks, rows, columns = value.shape
    for bit in order:
        mine = lax.rem(lax.div(here, bit), 2)
        value = value.reshape(2, -1, rows, columns)
        sent = lax.dynamic_index_in_dim(value, 1 - mine, 0, keepdims=False)
        (got,) = yield [cross(sent, bit)]
        own = lax.dynamic_index_in_dim(value, mine, 0, keepdims=False)
        value = (own.astype(F32) + got.astype(F32)).astype(BF16)
    value = value[0] if turn is None else (yield from turn(value[0]))
    value = value[None]
    for bit in order[::-1]:
        low = lax.rem(lax.div(here, bit), 2) == 0
        (got,) = yield [cross(value, bit)]
        value = jnp.concatenate([jnp.where(low, value, got), jnp.where(low, got, value)], 0)
    return value


class Rounds:
    def __init__(self):
        self.going = {}
        self.arriving = {}
        self.done = {}

    def add(self, name, task):
        self.going[name] = task
        self.arriving[name] = None
        self.step(name)

    def step(self, *names):
        for name in names:
            try:
                self.arriving[name] = self.going[name].send(self.arriving[name])
            except StopIteration as end:
                self.done[name] = end.value
                del self.going[name], self.arriving[name]

    def meet(self, values, *names):
        values, got = lax.optimization_barrier((values, [self.arriving[name] for name in names]))
        self.arriving.update(zip(names, got))
        self.step(*names)
        return values


def total_small(value):
    for flip in (1, 2):
        (got,) = yield [swap(value, flip)]
        value = value + got
    bit = 1
    while bit < lax.axis_size("rep"):
        (got,) = yield [cross(value, bit)]
        value = value + got
        bit *= 2
    return value


def dot(a, b, contract):
    return lax.dot_general(a, b, ((contract[:1], contract[1:]), ((), ())), preferred_element_type=F32)


def row_blocks(length, rows):
    return [slice(start, start + rows) for start in range(0, length, rows)]


def attend_kernel(
    me_ref, first_ref, into_ref, bias_ref, back_ref, mixed_ref, out_ref, part_ref, *, head, blocks
):
    me = me_ref[0]
    length, width = out_ref.shape
    rows = length // blocks
    scale = head**-0.5
    for block in row_blocks(length, rows):
        mixed_ref[block] = (dot(first_ref[block], into_ref[...], (1, 0)) + bias_ref[...]).astype(BF16)
    which = lax.broadcasted_iota(jnp.int32, (rows, LANES), 1) // head
    below = lax.broadcasted_iota(jnp.int32, (rows, rows), 1) <= lax.broadcasted_iota(
        jnp.int32, (rows, rows), 0
    )
    for pair in range(width // LANES):
        column = pair * LANES

        def block(index, part):
            start = pl.multiple_of((me ^ index) * rows, rows)
            return mixed_ref[pl.ds(start, rows), part * width + column : part * width + column + LANES]

        keys = [block(j, 1) for j in range(blocks)]
        values = [block(j, 2) for j in range(blocks)]
        for i in range(blocks):
            query = block(i, 0) * jnp.asarray(scale, BF16)
            result = jnp.zeros((rows, LANES), F32)
            for h in range(LANES // head):
                mine = jnp.where(which == h, query, jnp.zeros_like(query))
                scores = [dot(mine, keys[j], (1, 1)) for j in range(i + 1)]
                scores[i] = jnp.where(below, scores[i], -1e30)
                top = functools.reduce(
                    jnp.maximum, [jnp.max(s, 1, keepdims=True) for s in scores]
                )
                exps = [jnp.exp(s - top) for s in scores]
                total = sum(jnp.sum(e, 1, keepdims=True) for e in exps)
                acc = sum(dot(e.astype(BF16), values[j], (1, 0)) for j, e in enumerate(exps))
                result = jnp.where(which == h, acc / total, result)
            start = pl.multiple_of((me ^ i) * rows, rows)
            out_ref[pl.ds(start, rows), column : column + LANES] = result.astype(BF16)
    for block in row_blocks(length, rows):
        part_ref[block] = dot(out_ref[block], back_ref[...], (1, 0)).astype(BF16)


def attend_back_kernel(
    me_ref, mixed_ref, branch_ref, back_ref, into_ref, out_ref, part_ref, sums_ref, grad_ref, *, head, blocks
):
    me = me_ref[0]
    length, width = grad_ref.shape
    rows = length // blocks
    scale = head**-0.5
    for block in row_blocks(length, rows):
        grad_ref[block] = dot(branch_ref[block], back_ref[...], (1, 1)).astype(BF16)
    which = lax.broadcasted_iota(jnp.int32, (rows, LANES), 1) // head
    above = lax.broadcasted_iota(jnp.int32, (rows, rows), 0) <= lax.broadcasted_iota(
        jnp.int32, (rows, rows), 1
    )
    for pair in range(width // LANES):
        column = pair * LANES

        def place(index):
            return pl.ds(pl.multiple_of((me ^ index) * rows, rows), rows)

        def block(index, part):
            return mixed_ref[place(index), part * width + column : part * width + column + LANES]

        keys = [block(j, 1) for j in range(blocks)]
        values = [block(j, 2) for j in range(blocks)]
        d_keys = [jnp.zeros((rows, LANES), F32) for _ in range(blocks)]
        d_values = [jnp.zeros((rows, LANES), F32) for _ in range(blocks)]
        for i in range(blocks):
            query = block(i, 0) * jnp.asarray(scale, BF16)
            grad = grad_ref[place(i), column : column + LANES]
            d_query = jnp.zeros((rows, LANES), F32)
            for h in range(LANES // head):
                mine = jnp.where(which == h, query, jnp.zeros_like(query))
                mine_grad = jnp.where(which == h, grad, jnp.zeros_like(grad))
                scores = [dot(keys[j], mine, (1, 1)) for j in range(i + 1)]
                scores[i] = jnp.where(above, scores[i], -1e30)
                top = functools.reduce(
                    jnp.maximum, [jnp.max(s, 0, keepdims=True) for s in scores]
                )
                exps = [jnp.exp(s - top) for s in scores]
                inverse = 1.0 / sum(jnp.sum(e, 0, keepdims=True) for e in exps)
                probs = [e * inverse for e in exps]
                d_probs = [dot(values[j], mine_grad, (1, 1)) for j in range(i + 1)]
                inner = sum(jnp.sum(p * g, 0, keepdims=True) for p, g in zip(probs, d_probs))
                found = jnp.zeros((rows, LANES), F32)
                for j in range(i + 1):
                    d_score = (probs[j] * (d_probs[j] - inner)).astype(BF16)
                    d_keys[j] = d_keys[j] + dot(d_score, mine, (1, 0))
                    d_values[j] = d_values[j] + dot(probs[j].astype(BF16), mine_grad, (1, 0))
                    found = found + dot(d_score, keys[j], (0, 0))
                d_query = jnp.where(which == h, found, d_query)
            out_ref[place(i), column : column + LANES] = (d_query * scale).astype(BF16)
        for j in range(blocks):
            out_ref[place(j), width + column : width + column + LANES] = d_keys[j].astype(BF16)
            out_ref[place(j), 2 * width + column : 2 * width + column + LANES] = d_values[j].astype(BF16)
    total = jnp.zeros(sums_ref.shape, F32)
    for block in row_blocks(length, rows):
        mixed = out_ref[block]
        total = total + jnp.sum(mixed.astype(F32), 0, keepdims=True)
        part_ref[block] = dot(mixed, into_ref[...], (1, 1)).astype(BF16)
    sums_ref[...] = total


def feed_kernel(second_ref, up_ref, bias_ref, down_ref, active_ref, slope_ref, part_ref, *, blocks):
    length = second_ref.shape[0]
    root, cube = (2.0 / math.pi) ** 0.5, 0.044715
    for block in row_blocks(length, length // blocks):
        u = dot(second_ref[block], up_ref[...], (1, 0)) + bias_ref[...]
        t = jnp.tanh(root * (u + cube * u * u * u))
        active = (0.5 * u * (1.0 + t)).astype(BF16)
        active_ref[block] = active
        slope = 0.5 * (1.0 + t) + 0.5 * u * (1.0 - t * t) * root * (1.0 + 3.0 * cube * u * u)
        slope_ref[block] = slope.astype(BF16)
        part_ref[block] = dot(active, down_ref[...], (1, 0)).astype(BF16)


def feed_back_kernel(
    grad_ref, slope_ref, down_ref, up_ref, raised_ref, part_ref, sums_ref, *, blocks
):
    length = grad_ref.shape[0]
    total = jnp.zeros(sums_ref.shape, F32)
    for block in row_blocks(length, length // blocks):
        d_active = dot(grad_ref[block], down_ref[...], (1, 1))
        d_raised = (slope_ref[block].astype(F32) * d_active).astype(BF16)
        raised_ref[block] = d_raised
        total = total + jnp.sum(d_raised.astype(F32), 0, keepdims=True)
        part_ref[block] = dot(d_raised, up_ref[...], (1, 1)).astype(BF16)
    sums_ref[...] = total


def weights_kernel(*refs, blocks):
    out_ref = refs[-1]
    rows = out_ref.shape[0] // blocks
    start = 0
    for a_ref, b_ref in zip(refs[:-1:2], refs[1:-1:2]):
        size = b_ref.shape[1]
        for block in row_blocks(out_ref.shape[0], rows):
            out_ref[block, start : start + size] = dot(a_ref[:, block], b_ref[...], (0, 0)).astype(BF16)
        start += size


def kernel_call(kernel, arrays, outs, me=None, scratch=(), **sizes):
    scalars = [] if me is None else [jnp.reshape(me, (1,)).astype(jnp.int32)]
    return pl.pallas_call(
        functools.partial(kernel, **sizes),
        out_shape=[jax.ShapeDtypeStruct(shape, dtype) for shape, dtype in outs],
        in_specs=[pl.BlockSpec(memory_space=pltpu.SMEM)] * len(scalars)
        + [pl.BlockSpec(memory_space=pltpu.VMEM)] * len(arrays),
        out_specs=[pl.BlockSpec(memory_space=pltpu.VMEM)] * len(outs),
        scratch_shapes=list(scratch),
        compiler_params=pltpu.CompilerParams(vmem_limit_bytes=40 * 2**20),
        cost_estimate=pl.CostEstimate(flops=0, bytes_accessed=0, transcendentals=0),
    )(*scalars, *arrays)


def weight_products(*pairs, blocks):
    outs = [((pairs[0][0].shape[1], sum(b.shape[1] for _, b in pairs)), BF16)]
    return kernel_call(weights_kernel, [x for pair in pairs for x in pair], outs, blocks=blocks)[0]


def normed(values):
    average = jnp.mean(values, -1, keepdims=True)
    centered = values - average
    spread_of = jnp.mean(centered * centered, -1, keepdims=True)
    rate = lax.rsqrt(spread_of + 1e-05)
    return centered * rate, rate


def norm_back(incoming, values, gain):
    hat, rate = normed(values)
    scaled = incoming * gain
    first = jnp.mean(scaled, -1, keepdims=True)
    second = jnp.mean(scaled * hat, -1, keepdims=True)
    d_gain = jnp.sum(incoming * hat, 0)
    d_shift = jnp.sum(incoming, 0)
    return rate * (scaled - first - hat * second), d_gain, d_shift


def gelu_tanh(values):
    return jax.nn.gelu(values, approximate=True)


def shards(
    inputs,
    project_in,
    project_out,
    expand,
    contract,
    norm_gain,
    norm_shift,
    branch_bias,
    expand_bias,
    cotangent,
):
    layers = project_in.shape[0]
    rows, width = inputs.shape[1:]
    groups = lax.axis_size("grp")
    replicas = lax.axis_size("rep")
    head = width // HEADS
    part = width // groups
    hidden_part = expand.shape[2] // groups
    me = lax.axis_index("grp")
    replica = lax.axis_index("rep")

    def columns_by_device(weight, pieces):
        wide = weight.shape[1] // pieces
        size = wide // groups
        return jnp.stack(
            [
                jnp.concatenate(
                    [
                        weight[:, piece * wide + device * size : piece * wide + (device + 1) * size]
                        for piece in range(pieces)
                    ],
                    1,
                )
                for device in range(groups)
            ]
        )

    in_columns = [None] * layers
    up_columns = [None] * layers
    slice_rows = part // replicas

    def slices_by_device(weight, pieces):
        mine = lax.dynamic_slice_in_dim(weight, replica * slice_rows, slice_rows, 0)
        return columns_by_device(mine, pieces)

    def from_replicas(value):
        whole = lax.all_gather(value, "rep", axis=1, tiled=True)
        return whole.reshape(width, value.shape[-1])

    sent = slices_by_device(expand[0], 1)
    slice_up = at_once(exchange(sent, me))
    up_columns[0] = from_replicas(slice_up)
    sent = columns_by_device(tied([project_in[0]], sent)[0], 3)
    in_columns[0] = at_once(exchange(sent, me)).reshape(width, 3 * part)
    in_columns[0] = tied([in_columns[0]], slice_up)[0]
    slices = []
    for index in range(1, layers):
        pair = [slices_by_device(project_in[index], 3), slices_by_device(expand[index], 1)]
        both = at_once(exchange(tied([jnp.concatenate(pair, -1)], sent)[0], me))
        slices.append((both[..., : 3 * part], both[..., 3 * part :]))

    small = jnp.concatenate([norm_gain, norm_shift, branch_bias[:, 2:]], 1)
    small = lax.all_gather(small, "grp", axis=2, tiled=True).astype(F32)
    gains, shifts, out_biases = small[:, 0:2], small[:, 2:4], small[:, 4:6]
    mix_bias = jnp.concatenate(
        [branch_bias[:, 0], jnp.zeros_like(branch_bias[:, 0]), branch_bias[:, 1]], -1
    ).astype(F32)
    up_bias = expand_bias.astype(F32)

    state = inputs[0]
    saved = []
    for index in range(layers):
        hat, _ = normed(state)
        first = spread((hat * gains[index, 0] + shifts[index, 0]).astype(BF16))
        length = first.shape[0]
        mixed, attended, branch = kernel_call(
            attend_kernel,
            [first, in_columns[index], mix_bias[index : index + 1], project_out[index]],
            [((length, 3 * part), BF16), ((length, part), BF16), ((length, width), BF16)],
            me=me,
            head=head,
            blocks=groups,
        )
        if index < layers - 1:
            in_columns[index + 1] = from_replicas(tied([slices[index][0]], attended)[0])
        middle = state + collect(branch) + out_biases[index, 0]
        hat, _ = normed(middle)
        second = spread((hat * gains[index, 1] + shifts[index, 1]).astype(BF16))
        active, slope, down = kernel_call(
            feed_kernel,
            [second, up_columns[index], up_bias[index : index + 1], contract[index]],
            [((length, hidden_part), BF16)] * 2 + [((length, width), BF16)],
            blocks=groups,
        )
        if index < layers - 1:
            up_columns[index + 1] = from_replicas(tied([slices[index][1]], active)[0])
            state_after = middle + collect(down) + out_biases[index, 1]
        saved.append((state, first, mixed, attended, middle, second, slope, active, down))
        if index < layers - 1:
            state = state_after


    rounds = Rounds()

    def by_replica(value):
        cut = value.reshape(groups, replicas, slice_rows, value.shape[1])
        return cut.transpose(1, 0, 2, 3).reshape(replicas, groups * slice_rows, -1)

    def turn(value):
        got = yield from exchange(value.reshape(groups, -1, value.shape[-1]), me)
        return got.reshape(value.shape)

    def turn_both(value):
        turned = yield from turn(value[:, : 3 * part])
        return jnp.concatenate([turned, value[:, 3 * part :]], 1)

    bits = replica_bits()
    def feed_back(index, grad):
        second, slope, active = saved[index][5:8]
        d_down_own = grad.astype(BF16)
        d_down = spread(d_down_own)
        d_raised, partial, d_up_bias = kernel_call(
            feed_back_kernel,
            [d_down, slope, contract[index], up_columns[index]],
            [((length, hidden_part), BF16), ((length, width), BF16), ((1, hidden_part), F32)],
            blocks=groups,
        )
        early = tied([active, second], partial)
        g_contract = weight_products((early[0], d_down), blocks=groups)
        g_expand = weight_products((early[1], d_raised), blocks=groups)
        return g_contract, g_expand, (grad, d_down_own, partial, d_up_bias, g_expand)

    def norm_two_back(index, kept):
        grad, d_down_own, partial, d_up_bias, made = kept
        middle = saved[index][4]
        d_second = tied([collect(partial)], made)[0]
        d_middle, d_gain, d_shift = norm_back(d_second, middle, gains[index, 1])
        d_middle = grad + d_middle
        d_branch_own = d_middle.astype(BF16)
        sums = [jnp.sum(value.astype(F32), 0) for value in (d_branch_own, d_down_own)]
        return d_middle, spread(d_branch_own), [d_gain, d_shift] + sums, d_up_bias

    def attend_back(index, kept):
        d_middle, d_branch, (d_gain_two, d_shift_two, *sums), d_up_bias = kept
        before, first, mixed, attended, middle = saved[index][:5]
        state = None
        d_mixed, partial, d_mix_bias = kernel_call(
            attend_back_kernel,
            [mixed, d_branch, project_out[index], in_columns[index]],
            [((length, 3 * part), BF16), ((length, width), BF16), ((1, 3 * part), F32)],
            me=me,
            scratch=[pltpu.VMEM((length, part), BF16)],
            head=head,
            blocks=groups,
        )
        if index == layers - 1:
            down = tied([saved[index][8]], d_branch)[0]
            state = middle + collect(down) + out_biases[index, 1]
            partial = tied([partial], state)[0]
        early = tied([first, attended], partial)
        g_both = weight_products((early[0], d_mixed), (d_branch, early[1]), blocks=groups)
        d_first = tied([collect(partial)], g_both)[0]
        d_first, d_gain_one, d_shift_one = norm_back(d_first, before, gains[index, 0])
        own_rows = jnp.stack([d_gain_one, d_gain_two, d_shift_one, d_shift_two] + sums)
        own_part = jnp.concatenate([d_mix_bias[0, :part], d_mix_bias[0, 2 * part :], d_up_bias[0]])
        return g_both, (own_rows, own_part), d_middle + d_first, state

    def segment(run):
        shapes = jax.eval_shape(run)
        return lax.cond(
            replica < 4 * replicas,
            run,
            lambda: jax.tree.map(lambda leaf: jnp.zeros(leaf.shape, leaf.dtype), shapes),
        )

    def start_both(index, g_both):
        rounds.add("both %d" % index, replica_sum(by_replica(g_both), turn_both, bits))

    last = layers - 1
    small = [None] * layers
    g_contract, g_expand, kept = feed_back(last, cotangent[0])
    beside = lax.psum((g_contract, g_expand), "rep")

    def first_segment():
        g_both, small, grad, state = attend_back(last, norm_two_back(last, kept))
        return (g_both, small, state) + feed_back(0, grad)

    g_late, small[last], state, g_contract, g_expand, kept = segment(first_segment)
    rounds.add("contract 0", replica_sum(g_contract.reshape(replicas, -1, width), None, bits))
    kept = segment(lambda: norm_two_back(0, kept))
    kept, beside = lax.optimization_barrier((kept, beside))
    kept = rounds.meet(kept, "contract 0")
    rounds.add("expand 0", replica_sum(by_replica(g_expand), turn, bits))
    rounds.add("both 1", replica_sum(by_replica(g_late), turn_both, bits))
    g_both, small[0], grad, _ = segment(lambda: attend_back(0, kept))
    g_both = rounds.meet(g_both, "contract 0", "expand 0", "both 1")
    rounds.add("both 0", replica_sum(by_replica(g_both), turn_both, bits))
    rounds.done["contract 1"] = beside[0]
    rounds.add("expand 1", turn(beside[1]))

    whole = jnp.stack([item[0] for item in small])
    owned = jnp.stack([item[1] for item in small])
    owned_all = jnp.zeros((groups,) + owned.shape, F32)
    owned_all = lax.dynamic_update_index_in_dim(owned_all, owned, me, 0)
    rounds.step("contract 0", "expand 0", "both 1")
    both_small = tied([whole.reshape(-1), owned_all.reshape(-1)], rounds.arriving["expand 0"][0])
    rounds.add("small", total_small(jnp.concatenate(both_small)))
    while rounds.going:
        rounds.step(*rounds.going)

    grads = []
    for index in range(layers):
        g_contract, g_expand, g_both = [
            rounds.done["%s %d" % (name, index)] for name in ("contract", "expand", "both")
        ]

        def rows_from(value, source):
            if value.ndim == 2:
                return value[source * part : (source + 1) * part]
            return value.reshape(replicas, groups, slice_rows, -1)[:, source].reshape(part, -1)

        parts = [rows_from(g_both, source) for source in range(groups)]
        g_in = jnp.concatenate(
            [piece[:, kind * part : (kind + 1) * part] for kind in range(3) for piece in parts], 1
        )
        g_out = jnp.concatenate([piece[:, 3 * part :] for piece in parts], 0).T
        g_expand = jnp.concatenate([rows_from(g_expand, source) for source in range(groups)], 1)
        g_contract = g_contract.reshape(-1, width)
        each = (g_in, g_out, g_expand, g_contract)
        grads.append([lax.optimization_barrier(value) for value in each])

    summed = rounds.done["small"]
    whole = summed[: whole.size].reshape(whole.shape)
    whole = lax.dynamic_slice_in_dim(whole, me * part, part, 2)
    owned = lax.dynamic_index_in_dim(
        summed[-owned_all.size :].reshape(owned_all.shape), me, 0, keepdims=False
    )
    merged = [
        jnp.stack([grads[index][member] for index in range(layers)]).astype(F32)
        for member in range(4)
    ]
    bias_grad = jnp.concatenate(
        [owned[:, None, :part], owned[:, None, part : 2 * part], whole[:, 4:6]], 1
    )
    return (
        state[None],
        grad[None],
        merged[0],
        merged[1],
        merged[2],
        merged[3],
        whole[:, 0:2],
        whole[:, 2:4],
        bias_grad,
        owned[:, 2 * part :],
    )


def solution(mesh):
    placed = (
        P("rep", "grp", None),
        P(None, "grp", None),
        P(None, "grp", None),
        P(None, "grp", None),
        P(None, "grp", None),
        P(None, None, "grp"),
        P(None, None, "grp"),
        P(None, None, "grp"),
        P(None, "grp"),
        P("rep", "grp", None),
    )
    return jax.shard_map(
        shards,
        mesh=mesh,
        in_specs=placed,
        out_specs=(
            P("rep", "grp", None),
            P("rep", "grp", None),
            P(None, "grp", None),
            P(None, "grp", None),
            P(None, "grp", None),
            P(None, "grp", None),
            P(None, None, "grp"),
            P(None, None, "grp"),
            P(None, None, "grp"),
            P(None, "grp"),
        ),
        check_vma=False,
    )
```

```python
import functools
import math

import jax
import jax.numpy as jnp
from jax import lax
from jax.experimental import pallas as pl
from jax.experimental.pallas import tpu as pltpu
from jax.sharding import PartitionSpec as P

HEADS = 16
LANES = 128
F32 = jnp.float32
BF16 = jnp.bfloat16


def swap(value, flip):
    count = lax.axis_size("grp")
    return lax.ppermute(value, "grp", [(i, i ^ flip) for i in range(count)])


def spread(block):
    far = swap(block, 2)
    near = swap(block, 1)
    return jnp.concatenate([block, near, far, swap(far, 1)], 0)


def spread_rounds(block):
    (far,) = yield [swap(block, 2)]
    return jnp.concatenate([block, swap(block, 1), far, swap(far, 1)], 0)


def collect(parts):
    rows = parts.shape[0] // 4
    parts = parts.reshape(4, rows, parts.shape[1])
    got_far = swap(parts[3], 1)
    far = (parts[2].astype(F32) + got_far.astype(F32)).astype(BF16)
    got = swap(far, 2)
    near = swap(parts[1], 1)
    return parts[0].astype(F32) + near.astype(F32) + got.astype(F32)


def exchange(value, me):
    got = [
        swap(lax.dynamic_index_in_dim(value, me ^ r, 0, keepdims=False), r)
        for r in range(1, lax.axis_size("grp"))
    ]
    got = yield got
    out = value
    for r, block in enumerate(got, 1):
        out = lax.dynamic_update_index_in_dim(out, block, me ^ r, 0)
    return out


def at_once(task):
    try:
        got = next(task)
        while True:
            got = task.send(got)
    except StopIteration as end:
        return end.value


def cross(value, bit):
    count = lax.axis_size("rep")
    return lax.ppermute(value, "rep", [(i, i ^ bit) for i in range(count)])


def tied(values, anchor):
    if anchor is None:
        return values
    return list(lax.optimization_barrier(tuple(values) + (anchor,))[:-1])


def replica_bits():
    count = lax.axis_size("rep")
    bits = [1]
    while 2 * bits[-1] < count:
        bits.append(2 * bits[-1])
    return bits


def replica_sum(value, turn, order):
    here = lax.axis_index("rep")
    chunks, rows, columns = value.shape
    for bit in order:
        mine = lax.rem(lax.div(here, bit), 2)
        value = value.reshape(2, -1, rows, columns)
        sent = lax.dynamic_index_in_dim(value, 1 - mine, 0, keepdims=False)
        (got,) = yield [cross(sent, bit)]
        own = lax.dynamic_index_in_dim(value, mine, 0, keepdims=False)
        value = (own.astype(F32) + got.astype(F32)).astype(BF16)
    value = value[0] if turn is None else (yield from turn(value[0]))
    value = value[None]
    for bit in order[::-1]:
        low = lax.rem(lax.div(here, bit), 2) == 0
        (got,) = yield [cross(value, bit)]
        value = jnp.concatenate([jnp.where(low, value, got), jnp.where(low, got, value)], 0)
    return value


class Rounds:
    def __init__(self):
        self.going = {}
        self.arriving = {}
        self.done = {}

    def add(self, name, task):
        self.going[name] = task
        self.arriving[name] = None
        self.step(name)

    def step(self, *names):
        for name in names:
            try:
                self.arriving[name] = self.going[name].send(self.arriving[name])
            except StopIteration as end:
                self.done[name] = end.value
                del self.going[name], self.arriving[name]

    def meet(self, values, *names):
        values, got = lax.optimization_barrier((values, [self.arriving[name] for name in names]))
        self.arriving.update(zip(names, got))
        self.step(*names)
        return values


def total_small(value):
    for flip in (1, 2):
        (got,) = yield [swap(value, flip)]
        value = value + got
    bit = 1
    while bit < lax.axis_size("rep"):
        (got,) = yield [cross(value, bit)]
        value = value + got
        bit *= 2
    return value


def dot(a, b, contract):
    return lax.dot_general(a, b, ((contract[:1], contract[1:]), ((), ())), preferred_element_type=F32)


def row_blocks(length, rows):
    return [slice(start, start + rows) for start in range(0, length, rows)]


def attend_kernel(
    me_ref, first_ref, into_ref, bias_ref, back_ref, mixed_ref, out_ref, part_ref, *, head, blocks
):
    me = me_ref[0]
    length, width = out_ref.shape
    rows = length // blocks
    scale = head**-0.5
    for block in row_blocks(length, rows):
        mixed_ref[block] = (dot(first_ref[block], into_ref[...], (1, 0)) + bias_ref[...]).astype(BF16)
    which = lax.broadcasted_iota(jnp.int32, (rows, LANES), 1) // head
    below = lax.broadcasted_iota(jnp.int32, (rows, rows), 1) <= lax.broadcasted_iota(
        jnp.int32, (rows, rows), 0
    )
    for pair in range(width // LANES):
        column = pair * LANES

        def block(index, part):
            start = pl.multiple_of((me ^ index) * rows, rows)
            return mixed_ref[pl.ds(start, rows), part * width + column : part * width + column + LANES]

        keys = [block(j, 1) for j in range(blocks)]
        values = [block(j, 2) for j in range(blocks)]
        for i in range(blocks):
            query = block(i, 0) * jnp.asarray(scale, BF16)
            result = jnp.zeros((rows, LANES), F32)
            for h in range(LANES // head):
                mine = jnp.where(which == h, query, jnp.zeros_like(query))
                scores = [dot(mine, keys[j], (1, 1)) for j in range(i + 1)]
                scores[i] = jnp.where(below, scores[i], -1e30)
                top = functools.reduce(
                    jnp.maximum, [jnp.max(s, 1, keepdims=True) for s in scores]
                )
                exps = [jnp.exp(s - top) for s in scores]
                total = sum(jnp.sum(e, 1, keepdims=True) for e in exps)
                acc = sum(dot(e.astype(BF16), values[j], (1, 0)) for j, e in enumerate(exps))
                result = jnp.where(which == h, acc / total, result)
            start = pl.multiple_of((me ^ i) * rows, rows)
            out_ref[pl.ds(start, rows), column : column + LANES] = result.astype(BF16)
    for block in row_blocks(length, rows):
        part_ref[block] = dot(out_ref[block], back_ref[...], (1, 0)).astype(BF16)


def attend_back_kernel(
    me_ref, mixed_ref, branch_ref, back_ref, into_ref, out_ref, part_ref, sums_ref, grad_ref, *, head, blocks
):
    me = me_ref[0]
    length, width = grad_ref.shape
    rows = length // blocks
    scale = head**-0.5
    for block in row_blocks(length, rows):
        grad_ref[block] = dot(branch_ref[block], back_ref[...], (1, 1)).astype(BF16)
    which = lax.broadcasted_iota(jnp.int32, (rows, LANES), 1) // head
    above = lax.broadcasted_iota(jnp.int32, (rows, rows), 0) <= lax.broadcasted_iota(
        jnp.int32, (rows, rows), 1
    )
    for pair in range(width // LANES):
        column = pair * LANES

        def place(index):
            return pl.ds(pl.multiple_of((me ^ index) * rows, rows), rows)

        def block(index, part):
            return mixed_ref[place(index), part * width + column : part * width + column + LANES]

        keys = [block(j, 1) for j in range(blocks)]
        values = [block(j, 2) for j in range(blocks)]
        d_keys = [jnp.zeros((rows, LANES), F32) for _ in range(blocks)]
        d_values = [jnp.zeros((rows, LANES), F32) for _ in range(blocks)]
        for i in range(blocks):
            query = block(i, 0) * jnp.asarray(scale, BF16)
            grad = grad_ref[place(i), column : column + LANES]
            d_query = jnp.zeros((rows, LANES), F32)
            for h in range(LANES // head):
                mine = jnp.where(which == h, query, jnp.zeros_like(query))
                mine_grad = jnp.where(which == h, grad, jnp.zeros_like(grad))
                scores = [dot(keys[j], mine, (1, 1)) for j in range(i + 1)]
                scores[i] = jnp.where(above, scores[i], -1e30)
                top = functools.reduce(
                    jnp.maximum, [jnp.max(s, 0, keepdims=True) for s in scores]
                )
                exps = [jnp.exp(s - top) for s in scores]
                inverse = 1.0 / sum(jnp.sum(e, 0, keepdims=True) for e in exps)
                probs = [e * inverse for e in exps]
                d_probs = [dot(values[j], mine_grad, (1, 1)) for j in range(i + 1)]
                inner = sum(jnp.sum(p * g, 0, keepdims=True) for p, g in zip(probs, d_probs))
                found = jnp.zeros((rows, LANES), F32)
                for j in range(i + 1):
                    d_score = (probs[j] * (d_probs[j] - inner)).astype(BF16)
                    d_keys[j] = d_keys[j] + dot(d_score, mine, (1, 0))
                    d_values[j] = d_values[j] + dot(probs[j].astype(BF16), mine_grad, (1, 0))
                    found = found + dot(d_score, keys[j], (0, 0))
                d_query = jnp.where(which == h, found, d_query)
            out_ref[place(i), column : column + LANES] = (d_query * scale).astype(BF16)
        for j in range(blocks):
            out_ref[place(j), width + column : width + column + LANES] = d_keys[j].astype(BF16)
            out_ref[place(j), 2 * width + column : 2 * width + column + LANES] = d_values[j].astype(BF16)
    total = jnp.zeros(sums_ref.shape, F32)
    for block in row_blocks(length, rows):
        mixed = out_ref[block]
        total = total + jnp.sum(mixed.astype(F32), 0, keepdims=True)
        part_ref[block] = dot(mixed, into_ref[...], (1, 1)).astype(BF16)
    sums_ref[...] = total


def feed_kernel(second_ref, up_ref, bias_ref, down_ref, active_ref, slope_ref, part_ref, *, blocks):
    length = second_ref.shape[0]
    root, cube = (2.0 / math.pi) ** 0.5, 0.044715
    for block in row_blocks(length, length // blocks):
        u = dot(second_ref[block], up_ref[...], (1, 0)) + bias_ref[...]
        t = jnp.tanh(root * (u + cube * u * u * u))
        active = (0.5 * u * (1.0 + t)).astype(BF16)
        active_ref[block] = active
        slope = 0.5 * (1.0 + t) + 0.5 * u * (1.0 - t * t) * root * (1.0 + 3.0 * cube * u * u)
        slope_ref[block] = slope.astype(BF16)
        part_ref[block] = dot(active, down_ref[...], (1, 0)).astype(BF16)


def feed_back_kernel(
    grad_ref, slope_ref, down_ref, up_ref, raised_ref, part_ref, sums_ref, *, blocks
):
    length = grad_ref.shape[0]
    total = jnp.zeros(sums_ref.shape, F32)
    for block in row_blocks(length, length // blocks):
        d_active = dot(grad_ref[block], down_ref[...], (1, 1))
        d_raised = (slope_ref[block].astype(F32) * d_active).astype(BF16)
        raised_ref[block] = d_raised
        total = total + jnp.sum(d_raised.astype(F32), 0, keepdims=True)
        part_ref[block] = dot(d_raised, up_ref[...], (1, 1)).astype(BF16)
    sums_ref[...] = total


def weights_kernel(*refs, blocks):
    out_ref = refs[-1]
    rows = out_ref.shape[0] // blocks
    start = 0
    for a_ref, b_ref in zip(refs[:-1:2], refs[1:-1:2]):
        size = b_ref.shape[1]
        for block in row_blocks(out_ref.shape[0], rows):
            out_ref[block, start : start + size] = dot(a_ref[:, block], b_ref[...], (0, 0)).astype(BF16)
        start += size


def kernel_call(kernel, arrays, outs, me=None, scratch=(), **sizes):
    scalars = [] if me is None else [jnp.reshape(me, (1,)).astype(jnp.int32)]
    return pl.pallas_call(
        functools.partial(kernel, **sizes),
        out_shape=[jax.ShapeDtypeStruct(shape, dtype) for shape, dtype in outs],
        in_specs=[pl.BlockSpec(memory_space=pltpu.SMEM)] * len(scalars)
        + [pl.BlockSpec(memory_space=pltpu.VMEM)] * len(arrays),
        out_specs=[pl.BlockSpec(memory_space=pltpu.VMEM)] * len(outs),
        scratch_shapes=list(scratch),
        compiler_params=pltpu.CompilerParams(vmem_limit_bytes=40 * 2**20),
        cost_estimate=pl.CostEstimate(flops=0, bytes_accessed=0, transcendentals=0),
    )(*scalars, *arrays)


def weight_products(*pairs, blocks):
    outs = [((pairs[0][0].shape[1], sum(b.shape[1] for _, b in pairs)), BF16)]
    return kernel_call(weights_kernel, [x for pair in pairs for x in pair], outs, blocks=blocks)[0]


def normed(values):
    average = jnp.mean(values, -1, keepdims=True)
    centered = values - average
    spread_of = jnp.mean(centered * centered, -1, keepdims=True)
    rate = lax.rsqrt(spread_of + 1e-05)
    return centered * rate, rate


def norm_back(incoming, values, gain):
    hat, rate = normed(values)
    scaled = incoming * gain
    first = jnp.mean(scaled, -1, keepdims=True)
    second = jnp.mean(scaled * hat, -1, keepdims=True)
    d_gain = jnp.sum(incoming * hat, 0)
    d_shift = jnp.sum(incoming, 0)
    return rate * (scaled - first - hat * second), d_gain, d_shift


def gelu_tanh(values):
    return jax.nn.gelu(values, approximate=True)


def shards(
    inputs,
    project_in,
    project_out,
    expand,
    contract,
    norm_gain,
    norm_shift,
    branch_bias,
    expand_bias,
    cotangent,
):
    layers = project_in.shape[0]
    rows, width = inputs.shape[1:]
    groups = lax.axis_size("grp")
    replicas = lax.axis_size("rep")
    head = width // HEADS
    part = width // groups
    hidden_part = expand.shape[2] // groups
    me = lax.axis_index("grp")
    replica = lax.axis_index("rep")

    small = jnp.concatenate([norm_gain, norm_shift, branch_bias[:, 2:]], 1)
    small = lax.all_gather(small, "grp", axis=2, tiled=True).astype(F32)

    def columns_by_device(weight, pieces):
        wide = weight.shape[1] // pieces
        size = wide // groups
        return jnp.stack(
            [
                jnp.concatenate(
                    [
                        weight[:, piece * wide + device * size : piece * wide + (device + 1) * size]
                        for piece in range(pieces)
                    ],
                    1,
                )
                for device in range(groups)
            ]
        )

    in_columns = [None] * layers
    up_columns = [None] * layers
    slice_rows = part // replicas

    def slices_by_device(weight, pieces):
        mine = lax.dynamic_slice_in_dim(weight, replica * slice_rows, slice_rows, 0)
        return columns_by_device(mine, pieces)

    def from_replicas(value):
        whole = lax.all_gather(value, "rep", axis=1, tiled=True)
        return whole.reshape(width, value.shape[-1])

    sent = slices_by_device(tied([expand[0]], small)[0], 1)
    slice_up = at_once(exchange(sent, me))
    up_columns[0] = from_replicas(slice_up)
    sent = columns_by_device(tied([project_in[0]], sent)[0], 3)
    in_columns[0] = at_once(exchange(sent, me)).reshape(width, 3 * part)
    in_columns[0] = tied([in_columns[0]], slice_up)[0]
    gains, shifts, out_biases = small[:, 0:2], small[:, 2:4], small[:, 4:6]
    mix_bias = jnp.concatenate(
        [branch_bias[:, 0], jnp.zeros_like(branch_bias[:, 0]), branch_bias[:, 1]], -1
    ).astype(F32)
    up_bias = expand_bias.astype(F32)

    def segment(run):
        shapes = jax.eval_shape(run)
        return lax.cond(
            replica < 4 * replicas,
            run,
            lambda: jax.tree.map(lambda leaf: jnp.zeros(leaf.shape, leaf.dtype), shapes),
        )

    def start_both(index, g_both):
        rounds.add("both %d" % index, replica_sum(by_replica(g_both), turn_both, bits))

    state = inputs[0]
    saved = []
    hat, _ = normed(state)
    first = spread((hat * gains[0, 0] + shifts[0, 0]).astype(BF16))
    length = first.shape[0]
    rounds = Rounds()
    for index in range(1, layers):
        pair = [slices_by_device(project_in[index], 3), slices_by_device(expand[index], 1)]
        rounds.add(index, exchange(tied([jnp.concatenate(pair, -1)], sent)[0], me))
    cotangent_own = cotangent[0].astype(BF16)
    rounds.add("cotangent", spread_rounds(cotangent_own))
    for index in range(layers):

        def attend():
            mixed, attended, branch = kernel_call(
                attend_kernel,
                [first, in_columns[index], mix_bias[index : index + 1], project_out[index]],
                [((length, 3 * part), BF16), ((length, part), BF16), ((length, width), BF16)],
                me=me,
                head=head,
                blocks=groups,
            )
            middle = state + collect(branch) + out_biases[index, 0]
            hat, _ = normed(middle)
            second = spread((hat * gains[index, 1] + shifts[index, 1]).astype(BF16))
            return mixed, attended, middle, second

        def feed():
            return kernel_call(
                feed_kernel,
                [second, up_columns[index], up_bias[index : index + 1], contract[index]],
                [((length, hidden_part), BF16)] * 2 + [((length, width), BF16)],
                blocks=groups,
            )

        def feed_on():
            active, slope, down = feed()
            state = middle + collect(down) + out_biases[index, 1]
            hat, _ = normed(state)
            following = (hat * gains[index + 1, 0] + shifts[index + 1, 0]).astype(BF16)
            return active, slope, state, spread(following)

        before = state, first
        if index:
            mixed, attended, middle, second = attend()
        else:
            mixed, attended, middle, second = segment(attend)
            second = rounds.meet(second, *rounds.going)
        if index < layers - 1:
            down = None
            moved = rounds.done[index + 1]
            in_columns[index + 1] = from_replicas(moved[..., : 3 * part])
            active, slope, state, first = feed_on()
            up_columns[index + 1] = from_replicas(tied([moved[..., 3 * part :]], active)[0])
        else:
            active, slope, down = feed()
        saved.append((*before, mixed, attended, middle, second, slope, active, down))


    def by_replica(value):
        cut = value.reshape(groups, replicas, slice_rows, value.shape[1])
        return cut.transpose(1, 0, 2, 3).reshape(replicas, groups * slice_rows, -1)

    def turn(value):
        got = yield from exchange(value.reshape(groups, -1, value.shape[-1]), me)
        return got.reshape(value.shape)

    def turn_both(value):
        turned = yield from turn(value[:, : 3 * part])
        return jnp.concatenate([turned, value[:, 3 * part :]], 1)

    bits = replica_bits()
    def feed_back(index, grad, d_down=None):
        second, slope, active = saved[index][5:8]
        d_down_own = grad.astype(BF16)
        if d_down is None:
            d_down = spread(d_down_own)
        d_raised, partial, d_up_bias = kernel_call(
            feed_back_kernel,
            [d_down, slope, contract[index], up_columns[index]],
            [((length, hidden_part), BF16), ((length, width), BF16), ((1, hidden_part), F32)],
            blocks=groups,
        )
        early = tied([active, second], partial)
        g_contract = weight_products((early[0], d_down), blocks=groups)
        g_expand = weight_products((early[1], d_raised), blocks=groups)
        return g_contract, g_expand, (grad, d_down_own, partial, d_up_bias, g_expand)

    def norm_two_back(index, kept):
        grad, d_down_own, partial, d_up_bias, made = kept
        middle = saved[index][4]
        d_second = tied([collect(partial)], made)[0]
        d_middle, d_gain, d_shift = norm_back(d_second, middle, gains[index, 1])
        d_middle = grad + d_middle
        d_branch_own = d_middle.astype(BF16)
        sums = [jnp.sum(value.astype(F32), 0) for value in (d_branch_own, d_down_own)]
        return d_middle, spread(d_branch_own), [d_gain, d_shift] + sums, d_up_bias

    def attend_back(index, kept):
        d_middle, d_branch, (d_gain_two, d_shift_two, *sums), d_up_bias = kept
        before, first, mixed, attended, middle = saved[index][:5]
        state = None
        d_mixed, partial, d_mix_bias = kernel_call(
            attend_back_kernel,
            [mixed, d_branch, project_out[index], in_columns[index]],
            [((length, 3 * part), BF16), ((length, width), BF16), ((1, 3 * part), F32)],
            me=me,
            scratch=[pltpu.VMEM((length, part), BF16)],
            head=head,
            blocks=groups,
        )
        if index == layers - 1:
            down = tied([saved[index][8]], d_branch)[0]
            state = middle + collect(down) + out_biases[index, 1]
            partial = tied([partial], state)[0]
        early = tied([first, attended], partial)
        g_both = weight_products((early[0], d_mixed), (d_branch, early[1]), blocks=groups)
        d_first = tied([collect(partial)], g_both)[0]
        d_first, d_gain_one, d_shift_one = norm_back(d_first, before, gains[index, 0])
        own_rows = jnp.stack([d_gain_one, d_gain_two, d_shift_one, d_shift_two] + sums)
        own_part = jnp.concatenate([d_mix_bias[0, :part], d_mix_bias[0, 2 * part :], d_up_bias[0]])
        return g_both, (own_rows, own_part), d_middle + d_first, state

    last = layers - 1
    small = [None] * layers
    g_contract, g_expand, kept = feed_back(last, cotangent[0], rounds.done["cotangent"])
    beside = lax.psum((g_contract, g_expand), "rep")

    def first_segment():
        g_both, small, grad, state = attend_back(last, norm_two_back(last, kept))
        return (g_both, small, state) + feed_back(0, grad)

    g_late, small[last], state, g_contract, g_expand, kept = segment(first_segment)
    rounds.add("contract 0", replica_sum(g_contract.reshape(replicas, -1, width), None, bits))
    kept = segment(lambda: norm_two_back(0, kept))
    kept, beside = lax.optimization_barrier((kept, beside))
    kept = rounds.meet(kept, "contract 0")
    rounds.add("expand 0", replica_sum(by_replica(g_expand), turn, bits))
    rounds.add("both 1", replica_sum(by_replica(g_late), turn_both, bits))
    g_both, small[0], grad, _ = segment(lambda: attend_back(0, kept))
    g_both = rounds.meet(g_both, "contract 0", "expand 0", "both 1")
    rounds.add("both 0", replica_sum(by_replica(g_both), turn_both, bits))
    rounds.done["contract 1"] = beside[0]
    rounds.add("expand 1", turn(beside[1]))

    whole = jnp.stack([item[0] for item in small])
    owned = jnp.stack([item[1] for item in small])
    owned_all = jnp.zeros((groups,) + owned.shape, F32)
    owned_all = lax.dynamic_update_index_in_dim(owned_all, owned, me, 0)
    rounds.step("contract 0", "expand 0", "both 1")
    both_small = tied([whole.reshape(-1), owned_all.reshape(-1)], rounds.arriving["expand 0"][0])
    rounds.add("small", total_small(jnp.concatenate(both_small)))
    while rounds.going:
        rounds.step(*rounds.going)

    grads = []
    for index in range(layers):
        g_contract, g_expand, g_both = [
            rounds.done["%s %d" % (name, index)] for name in ("contract", "expand", "both")
        ]

        def rows_from(value, source):
            if value.ndim == 2:
                return value[source * part : (source + 1) * part]
            return value.reshape(replicas, groups, slice_rows, -1)[:, source].reshape(part, -1)

        parts = [rows_from(g_both, source) for source in range(groups)]
        g_in = jnp.concatenate(
            [piece[:, kind * part : (kind + 1) * part] for kind in range(3) for piece in parts], 1
        )
        g_out = jnp.concatenate([piece[:, 3 * part :] for piece in parts], 0).T
        g_expand = jnp.concatenate([rows_from(g_expand, source) for source in range(groups)], 1)
        g_contract = g_contract.reshape(-1, width)
        each = (g_in, g_out, g_expand, g_contract)
        grads.append([lax.optimization_barrier(value) for value in each])

    summed = rounds.done["small"]
    whole = summed[: whole.size].reshape(whole.shape)
    whole = lax.dynamic_slice_in_dim(whole, me * part, part, 2)
    owned = lax.dynamic_index_in_dim(
        summed[-owned_all.size :].reshape(owned_all.shape), me, 0, keepdims=False
    )
    merged = [
        jnp.stack([grads[index][member] for index in range(layers)]).astype(F32)
        for member in range(4)
    ]
    bias_grad = jnp.concatenate(
        [owned[:, None, :part], owned[:, None, part : 2 * part], whole[:, 4:6]], 1
    )
    return (
        state[None],
        grad[None],
        merged[0],
        merged[1],
        merged[2],
        merged[3],
        whole[:, 0:2],
        whole[:, 2:4],
        bias_grad,
        owned[:, 2 * part :],
    )


def solution(mesh):
    placed = (
        P("rep", "grp", None),
        P(None, "grp", None),
        P(None, "grp", None),
        P(None, "grp", None),
        P(None, "grp", None),
        P(None, None, "grp"),
        P(None, None, "grp"),
        P(None, None, "grp"),
        P(None, "grp"),
        P("rep", "grp", None),
    )
    return jax.shard_map(
        shards,
        mesh=mesh,
        in_specs=placed,
        out_specs=(
            P("rep", "grp", None),
            P("rep", "grp", None),
            P(None, "grp", None),
            P(None, "grp", None),
            P(None, "grp", None),
            P(None, "grp", None),
            P(None, None, "grp"),
            P(None, None, "grp"),
            P(None, None, "grp"),
            P(None, "grp"),
        ),
        check_vma=False,
    )
```
